32 devices in a mesh: groups: 2 (over x), param: 16 (over z, y, core).
Axes of the slice: x: 2, y: 2, z: 4, core: 2. Of those that a mesh axis runs over, the one named last changes fastest.
Arguments:
- gradients: bfloat16 [1024, 10240], P('groups', 'param'), parts along dimension 0
- proj_matrix: bfloat16 [10240, 8192], P('param')
- train_task: int32 [768], P('groups'), parts along dimension 0, may hold values from 0 to 11, as said below
- val_task: int32 [256], P('groups'), parts along dimension 0, may hold values from 0 to 7, as said below
- task_pairs: int32 [64, 2], P(('groups', 'param')), parts along dimension 0, may hold values from 0 to 11, as said below
- owner_slot: int32 [1024], P('groups'), parts along dimension 0, may hold values from 0 to 511, each once
Outputs:
- unit_rows: bfloat16 [1024, 8192], P(('groups', 'param')), parts along dimension 0
- tiles: float32 [64, 32, 16], P(('groups', 'param')), parts along dimension 0
- scores: float32 [1024], P(('groups', 'param')), parts along dimension 0
The draws below stay inside these ranges and needn't reach their ends.
There are 2 independent parts, one for each index of `groups`. The reference program is written for one: setup_inputs(seed, part) draws one part's arguments, and reference() takes and returns one part's arrays. A program takes and returns all parts, laid end to end along the dimension named above; an argument that names none is the same for every part. Nothing has to cross between parts.
Inputs may be any that keep to these rules, and one draw needn't show every extreme that they name: `train_task`: every training task holds exactly 32 examples. `val_task`: every validation task holds exactly 16 examples. `task_pairs`: column 0 is a training task, column 1 a validation task; every task appears; pairs may repeat.
All inputs are finite; a program needn't handle non-finite values.
Results may differ from the reference program's by a relative error of at most 0.0026.
Values may be sent and summed in bfloat16 or wider, within the bound.
A program may use at most 128 MiB of HBM per device.

```python
import jax
import jax.numpy as jnp
from jax import lax

PROJ_DIM = 8192
TRAIN_TASKS = 12
TRAIN_PER = 32
VAL_TASKS = 8
VAL_PER = 16
PARAMS = 10240
TRAIN = 384
VAL = 128
EXAMPLES = 512
NPAIR = 32


def task_lists(key):
    first_key, second_key = jax.random.split(key)
    train_ids = jax.random.permutation(first_key, jnp.arange(TRAIN, dtype=jnp.int32) // TRAIN_PER)
    val_ids = jax.random.permutation(second_key, jnp.arange(VAL, dtype=jnp.int32) // VAL_PER)
    return (train_ids.astype(jnp.int32), val_ids.astype(jnp.int32))


def draw_train_task(key, part):
    return task_lists(key)[0]


def draw_val_task(key, part):
    return task_lists(key)[1]


def draw_gradients(key, part):
    train_ids, val_ids = task_lists(key)
    key = jax.random.fold_in(key, 11)
    keys = jax.random.split(key, 6)
    task_index = jnp.concatenate([train_ids, val_ids + TRAIN_TASKS])
    task_coef = jax.random.normal(keys[0], (TRAIN_TASKS + VAL_TASKS, 16), jnp.float32)
    coef = task_coef[task_index] + 0.8 * jax.random.normal(keys[1], (EXAMPLES, 16), jnp.float32)
    basis = jax.random.normal(keys[2], (16, PARAMS), jnp.float32)
    shared = jnp.zeros((EXAMPLES, PARAMS), jnp.float32)
    for level in range(16):
        shared = shared + coef[:, level:level + 1] * basis[level][None, :]
    task_mean = jax.random.normal(keys[3], (TRAIN_TASKS + VAL_TASKS, PARAMS), jnp.float32)
    noise = jax.random.normal(keys[4], (EXAMPLES, PARAMS), jnp.float32)
    values = 0.25 * shared + 0.5 * task_mean[task_index] + 0.7 * noise
    row_scale = jnp.exp(jax.random.uniform(keys[5], (EXAMPLES, 1), jnp.float32, jnp.log(0.5), jnp.log(5.0)))
    return (values * row_scale * 0.01).astype(jnp.bfloat16)


def draw_proj_matrix(key, part):
    key = jax.random.fold_in(key, 5)
    first_key, second_key = jax.random.split(key)
    column_scale = jnp.exp(jax.random.uniform(first_key, (1, PROJ_DIM), jnp.float32, 0.0, jnp.log(10.0)))
    base = jax.random.normal(second_key, (PARAMS, PROJ_DIM), jnp.float32)
    return (base * column_scale * PARAMS ** (-0.5)).astype(jnp.bfloat16)


def draw_task_pairs(key, part):
    key = jax.random.fold_in(key, 3)
    first_key, second_key = jax.random.split(key)
    positions = jnp.arange(NPAIR, dtype=jnp.int32)
    train_side = jax.random.permutation(first_key, positions % TRAIN_TASKS)
    val_side = jax.random.permutation(second_key, positions % VAL_TASKS)
    return jnp.stack([train_side, val_side], axis=1).astype(jnp.int32)


def setup_inputs(seed: int = 0, part: int = 0) -> dict:
    key_of = jax.random.split(jax.random.key(seed), 7)
    part_keys = jax.random.split(jax.random.fold_in(key_of[6], part), 7)
    gradients = draw_gradients(jax.random.fold_in(jax.random.fold_in(key_of[6], part), 71), part)
    proj_matrix = draw_proj_matrix(jax.random.fold_in(key_of[6], 71), part)
    train_task = draw_train_task(jax.random.fold_in(jax.random.fold_in(key_of[6], part), 71), part)
    val_task = draw_val_task(jax.random.fold_in(jax.random.fold_in(key_of[6], part), 71), part)
    task_pairs = draw_task_pairs(jax.random.fold_in(jax.random.fold_in(key_of[6], part), 71), part)
    owner_slot = jax.random.permutation(part_keys[5], EXAMPLES).astype(jnp.int32)
    return {"gradients": gradients, "proj_matrix": proj_matrix, "train_task": train_task, "val_task": val_task, "task_pairs": task_pairs, "owner_slot": owner_slot}


epsilon = 1e-06

def reference(gradients, proj_matrix, train_task, val_task, task_pairs, owner_slot):
    projected = jnp.dot(gradients, proj_matrix, preferred_element_type=jnp.float32)
    squares = lax.optimization_barrier(jnp.sum(projected * projected, axis=1, keepdims=True))
    unit = (projected * lax.rsqrt(squares + epsilon)).astype(jnp.bfloat16)
    train_rows = jnp.argsort(train_task, stable=True).astype(jnp.int32).reshape(TRAIN_TASKS, TRAIN_PER)
    val_rows = (jnp.argsort(val_task, stable=True).astype(jnp.int32) + TRAIN).reshape(VAL_TASKS, VAL_PER)
    left_ids = train_rows[task_pairs[:, 0]]
    right_ids = val_rows[task_pairs[:, 1]]
    left_side = unit[left_ids].astype(jnp.float32)
    right_side = unit[right_ids].astype(jnp.float32)
    tiles = jnp.einsum('prk,pck->prc', left_side, right_side)
    per_example = jnp.zeros((EXAMPLES,), jnp.float32)
    per_example = per_example.at[left_ids].add(lax.optimization_barrier(jnp.mean(tiles, axis=2)))
    per_example = per_example.at[right_ids].add(lax.optimization_barrier(jnp.mean(tiles, axis=1)))
    unit_rows = jnp.zeros_like(unit).at[owner_slot].set(unit)
    scores = jnp.zeros((EXAMPLES,), jnp.float32).at[owner_slot].set(per_example)
    return (unit_rows, tiles, scores)
```

```python
import functools

import jax
import jax.numpy as jnp
from jax import lax
from jax.experimental import pallas as pl
from jax.experimental.pallas import tpu as pltpu
from jax.sharding import PartitionSpec as P

TRAIN_TASKS = 12
TRAIN_PER = 32
VAL_TASKS = 8
VAL_PER = 16
TRAIN = 384
VAL = 128
CORES = 2
YS = 2

epsilon = 1e-06
FULL = 32000.0


def row_scale(v):
    top = jnp.max(jnp.abs(v), axis=1, keepdims=True)
    return jnp.maximum(top, 1e-30)


def to_int16(v, top):
    return jnp.floor(v * (FULL / top) + 0.5).astype(jnp.int32).astype(jnp.int16)


def to_lanes(top):
    rows = top.shape[0]
    return jnp.transpose(jnp.broadcast_to(top * (1.0 / FULL), (rows, 128)))[0:1]


def to_rows(lanes):
    return jnp.transpose(jnp.broadcast_to(lanes, (128, 128)))


def kernel(
    zs, g_ref, s_ref, p_ref,
    unit_ref, gram_ref,
    p_buf, c_send, c_recv, y_own, y_send, y_recv, ys_send, ys_recv,
    z_send, z_recv, zs_send, zs_recv, acc, squares, turned,
    u_send, u_all, g_part, g_recv, g_sum,
    p_sem, cs_sem, cr_sem, yss_sem, ysr_sem, yds_sem, ydr_sem,
    zss_sem, zsr_sem, zds_sem, zdr_sem, us_sem, ur_sem, gs_sem, gr_sem, hs_sem, hr_sem,
):
    n = zs * YS * CORES
    chunks, rows, width = acc.shape
    me = lax.axis_index("param")
    core = lax.rem(me, CORES)
    y = lax.rem(lax.div(me, CORES), YS)
    z = lax.div(me, CORES * YS)
    sibling = me + 1 - 2 * core
    y_peer = me + CORES * (1 - 2 * y)
    half = g_ref.shape[0] // 2
    quarter = half // 2

    def load(k):
        return pltpu.make_async_copy(
            p_ref.at[:, pl.ds(pl.multiple_of(k * width, width), width)], p_buf.at[k], p_sem.at[k])

    def start_load(k, carry):
        load(k).start()
        return carry

    lax.fori_loop(0, chunks, start_load, 0)

    barrier = pltpu.get_barrier_semaphore()
    for j in range(1, n):
        pl.semaphore_signal(barrier, inc=1, device_id={"param": lax.rem(me + j, n)},
                            device_id_type=pl.DeviceIdType.MESH)
    pl.semaphore_wait(barrier, n - 1)

    def remote(src, dst, send, recv, to):
        return pltpu.make_async_remote_copy(
            src_ref=src, dst_ref=dst, send_sem=send, recv_sem=recv,
            device_id={"param": to}, device_id_type=pl.DeviceIdType.MESH)

    def core_copy(k):
        return remote(c_send.at[k], c_recv.at[k], cs_sem.at[k], cr_sem.at[k], sibling)

    def y_copies(k):
        return (remote(y_send.at[k], y_recv.at[k], yds_sem.at[k], ydr_sem.at[k], y_peer),
                remote(ys_send.at[k], ys_recv.at[k], yss_sem.at[k], ysr_sem.at[k], y_peer))

    def z_copies(k, j):
        zz = lax.rem(z + j, zs)
        to = zz * (CORES * YS) + y * CORES + core
        return (remote(z_send.at[k, zz], z_recv.at[k, j - 1], zds_sem.at[k, j - 1],
                       zdr_sem.at[k, j - 1], to),
                remote(zs_send.at[k], zs_recv.at[k, j - 1], zss_sem.at[k, j - 1],
                       zsr_sem.at[k, j - 1], to))

    squares[...] = jnp.zeros_like(squares)

    def step(t, carry):
        @pl.when(t < chunks)
        def _():
            k = t
            load(k).wait()
            theirs = g_ref[pl.ds(pl.multiple_of((1 - core) * half, half), half), :]
            c_send[k] = jnp.dot(theirs, p_buf[k], preferred_element_type=jnp.float32)
            core_copy(k).start()

        @pl.when(jnp.logical_and(t >= 1, t < chunks + 1))
        def _():
            k = t - 1
            away = pl.multiple_of((1 - y) * quarter, quarter)
            home = pl.multiple_of(y * quarter, quarter)
            base = core * half
            g_away = g_ref[pl.ds(pl.multiple_of(base + away, quarter), quarter), :]
            g_home = g_ref[pl.ds(pl.multiple_of(base + home, quarter), quarter), :]
            d_away = jnp.dot(g_away, p_buf[k], preferred_element_type=jnp.float32)
            d_home = jnp.dot(g_home, p_buf[k], preferred_element_type=jnp.float32)
            core_copy(k).wait_recv()
            v = d_away + c_recv[k, pl.ds(away, quarter), :]
            top = row_scale(v)
            y_send[k] = to_int16(v, top)
            ys_send[k] = to_lanes(top)
            for c in y_copies(k):
                c.start()
            y_own[k] = d_home + c_recv[k, pl.ds(home, quarter), :]

        @pl.when(jnp.logical_and(t >= 3, t < chunks + 3))
        def _():
            k = t - 3
            for c in y_copies(k):
                c.wait_recv()
            scale = to_rows(ys_recv[k])[:, 0:1]
            v = y_own[k] + y_recv[k].astype(jnp.int32).astype(jnp.float32) * scale
            top = row_scale(v)
            q = to_int16(v, top)
            z_send[k] = q.reshape(zs, rows, width)
            zs_send[k] = to_lanes(top)
            for j in range(1, zs):
                for c in z_copies(k, j):
                    c.start()
            y_own[k] = v
            acc[k] = y_own[k, pl.ds(pl.multiple_of(z * rows, rows), rows), :]

        @pl.when(t >= 5)
        def _():
            k = t - 5
            v = acc[k]
            for j in range(1, zs):
                for c in z_copies(k, j):
                    c.wait_recv()
                turned[...] = to_rows(zs_recv[k, j - 1])
                scale = turned[pl.ds(pl.multiple_of(z * rows, rows), rows), :][:, 0:1]
                v = v + z_recv[k, j - 1].astype(jnp.int32).astype(jnp.float32) * scale
            acc[k] = v
            squares[...] += jnp.sum(v * v, axis=1, keepdims=True)

        return carry

    lax.fori_loop(0, chunks + 5, step, 0)

    factor = lax.rsqrt(squares[...] + epsilon)[:, 0:1]
    for k in range(chunks):
        u = (acc[k] * factor).astype(jnp.bfloat16)
        unit_ref[:, k * width:(k + 1) * width] = u
        u_send[k] = u

    def u_copy(j):
        to = lax.rem(me + j, n)
        return remote(u_send.at[to], u_all.at[me], us_sem.at[j - 1], ur_sem.at[j - 1], to)

    for j in range(1, n):
        u_copy(j).start()
    u_all[me] = u_send[me]

    def drain(k, carry):
        core_copy(k).wait_send()
        for c in y_copies(k):
            c.wait_send()
        for j in range(1, zs):
            for c in z_copies(k, j):
                c.wait_send()
        return carry

    lax.fori_loop(0, chunks, drain, 0)
    for j in range(1, n):
        u_copy(j).wait()

    whole = u_all[...].reshape(n * rows, width)
    ordered = jnp.dot(s_ref[...], whole, preferred_element_type=jnp.float32).astype(jnp.bfloat16)
    gram = lax.dot_general(ordered[:TRAIN], ordered[TRAIN:], (((1,), (1,)), ((), ())),
                           preferred_element_type=jnp.float32)
    g_part[...] = gram.reshape(g_part.shape)

    def g_copy(j):
        to = lax.rem(me + j, n)
        return remote(g_part.at[to], g_recv.at[j - 1], gs_sem.at[j - 1], gr_sem.at[j - 1], to)

    for j in range(1, n):
        g_copy(j).start()
    total = g_part[me]
    for j in range(1, n):
        g_copy(j).wait_recv()
        total = total + g_recv[j - 1]
    g_sum[...] = total

    def h_copy(j):
        to = lax.rem(me + j, n)
        return remote(g_sum, gram_ref.at[me], hs_sem.at[j - 1], hr_sem.at[j - 1], to)

    for j in range(1, n):
        h_copy(j).start()
    gram_ref[me] = total
    for j in range(1, n):
        g_copy(j).wait_send()
        h_copy(j).wait()


def project(n, ordered, select, proj_matrix):
    zs = n // (CORES * YS)
    total, depth = ordered.shape
    cols = proj_matrix.shape[1]
    rows, width, chunks = total // n, cols // n, n
    half, quarter = total // 2, total // 4
    f32, bf16, i16 = jnp.float32, jnp.bfloat16, jnp.int16
    dma = pltpu.SemaphoreType.DMA
    part = TRAIN // n
    vmem = pl.BlockSpec(memory_space=pltpu.VMEM)
    return pl.pallas_call(
        functools.partial(kernel, zs),
        out_shape=(jax.ShapeDtypeStruct((rows, cols), bf16),
                   jax.ShapeDtypeStruct((n, part, VAL), f32)),
        in_specs=[vmem, vmem, pl.BlockSpec(memory_space=pl.ANY)],
        out_specs=(vmem, vmem),
        scratch_shapes=[
            pltpu.VMEM((chunks, depth, width), bf16),
            pltpu.VMEM((chunks, half, width), f32),
            pltpu.VMEM((chunks, half, width), f32),
            pltpu.VMEM((chunks, quarter, width), f32),
            pltpu.VMEM((chunks, quarter, width), i16),
            pltpu.VMEM((chunks, quarter, width), i16),
            pltpu.VMEM((chunks, 1, quarter), f32),
            pltpu.VMEM((chunks, 1, quarter), f32),
            pltpu.VMEM((chunks, zs, rows, width), i16),
            pltpu.VMEM((chunks, zs - 1, rows, width), i16),
            pltpu.VMEM((chunks, 1, quarter), f32),
            pltpu.VMEM((chunks, zs - 1, 1, quarter), f32),
            pltpu.VMEM((chunks, rows, width), f32),
            pltpu.VMEM((rows, 128), f32),
            pltpu.VMEM((128, 128), f32),
            pltpu.VMEM((n, rows, width), bf16),
            pltpu.VMEM((n, rows, width), bf16),
            pltpu.VMEM((n, part, VAL), f32),
            pltpu.VMEM((n - 1, part, VAL), f32),
            pltpu.VMEM((part, VAL), f32),
            dma((chunks,)),
            dma((chunks,)), dma((chunks,)),
            dma((chunks,)), dma((chunks,)), dma((chunks,)), dma((chunks,)),
            dma((chunks, zs - 1)), dma((chunks, zs - 1)),
            dma((chunks, zs - 1)), dma((chunks, zs - 1)),
            dma((n - 1,)), dma((n - 1,)), dma((n - 1,)), dma((n - 1,)),
            dma((n - 1,)), dma((n - 1,)),
        ],
        compiler_params=pltpu.CompilerParams(
            collective_id=0, has_side_effects=True, vmem_limit_bytes=60 * 2**20),
        cost_estimate=pl.CostEstimate(
            flops=2 * total * depth * cols, bytes_accessed=2 * depth * cols, transcendentals=0),
    )(ordered, select, proj_matrix)


def fused(n, gradients, proj_matrix, train_task, val_task, task_pairs, owner_slot):
    total = gradients.shape[0]
    rows = total // n
    zs = n // (CORES * YS)
    me = lax.axis_index("param")
    index = jnp.arange(total, dtype=jnp.int32)

    def place(task, per):
        i = jnp.arange(task.shape[0], dtype=jnp.int32)
        before = (task[None, :] == task[:, None]) & (i[None, :] < i[:, None])
        return task * per + jnp.sum(before.astype(jnp.int32), axis=1)

    spot = jnp.concatenate([place(train_task, TRAIN_PER), place(val_task, VAL_PER) + TRAIN])
    owns = owner_slot[None, :] == index[:, None]
    inverse = jnp.sum(jnp.where(owns, index[None, :], 0), axis=1)
    spot_of_slot = jnp.sum(jnp.where(owns, spot[None, :], 0), axis=1)
    select = (spot_of_slot[None, :] == index[:, None]).astype(jnp.bfloat16)
    order = inverse.reshape(zs, YS, CORES, rows).transpose(2, 1, 0, 3).reshape(total)
    every_pair = lax.all_gather(task_pairs, "param", axis=0, tiled=True)
    unit_rows, gram = project(n, gradients[order], select, proj_matrix)
    gram = gram.reshape(TRAIN, VAL)
    blocks = gram.reshape(TRAIN_TASKS, TRAIN_PER, VAL_TASKS, VAL_PER)
    tiles = blocks[task_pairs[:, 0], :, task_pairs[:, 1], :]
    a = jnp.arange(TRAIN, dtype=jnp.int32) // TRAIN_PER
    b = jnp.arange(VAL, dtype=jnp.int32) // VAL_PER
    hits = (every_pair[:, 0, None, None] == a[None, :, None]) & (
        every_pair[:, 1, None, None] == b[None, None, :])
    weighted = gram * jnp.sum(hits.astype(jnp.float32), axis=0)
    sums = jnp.concatenate([
        jnp.sum(weighted, axis=1) * (1.0 / VAL_PER), jnp.sum(weighted, axis=0) * (1.0 / TRAIN_PER)])
    mine = lax.dynamic_slice(spot_of_slot, (me * rows,), (rows,))
    scores = jnp.sum(jnp.where(mine[:, None] == index[None, :], sums[None, :], 0.0), axis=1)
    return (unit_rows, tiles, scores)


def shards(gradients, proj_matrix, train_task, val_task, task_pairs, owner_slot):
    total_rows = gradients.shape[0]
    inverse = (
        jnp.zeros((total_rows,), jnp.int32)
        .at[owner_slot]
        .set(jnp.arange(total_rows, dtype=jnp.int32))
    )
    ordered = gradients[inverse]
    owned = lax.psum_scatter(
        jnp.dot(ordered, proj_matrix, preferred_element_type=jnp.float32),
        "param",
        scatter_dimension=0,
        tiled=True,
    )
    squares = jnp.sum(owned * owned, axis=1, keepdims=True)
    unit_rows = (owned * lax.rsqrt(squares + epsilon)).astype(jnp.bfloat16)
    train_rows = jnp.argsort(train_task, stable=True).reshape(TRAIN_TASKS, TRAIN_PER)
    val_order = jnp.argsort(val_task, stable=True).reshape(VAL_TASKS, VAL_PER)
    left_slots = owner_slot[train_rows[task_pairs[:, 0]]]
    val_index = val_order[task_pairs[:, 1]]
    right_slots = owner_slot[val_index + TRAIN]
    every_unit = lax.all_gather(unit_rows, "param", axis=0, tiled=True)
    left_side = every_unit[left_slots]
    right_side = every_unit[right_slots]
    tiles = jnp.einsum("prk,pck->prc", left_side, right_side, preferred_element_type=jnp.float32)
    contrib = jnp.zeros((total_rows,), jnp.float32)
    contrib = contrib.at[left_slots].add(jnp.mean(tiles, axis=2))
    contrib = contrib.at[right_slots].add(jnp.mean(tiles, axis=1))
    scores = lax.psum_scatter(contrib, "param", scatter_dimension=0, tiled=True)
    return (unit_rows, tiles, scores)


def solution(mesh):
    in_specs = (
        P("groups", "param"),
        P("param", None),
        P("groups"),
        P("groups"),
        P(("groups", "param"), None),
        P("groups"),
    )
    out_specs = (
        P(("groups", "param"), None),
        P(("groups", "param"), None, None),
        P(("groups", "param")),
    )
    n = mesh.shape["param"]
    body = functools.partial(fused, n) if n == 16 else shards
    return jax.shard_map(body, mesh=mesh, in_specs=in_specs, out_specs=out_specs, check_vma=False)
```

```python
import functools

import jax
import jax.numpy as jnp
from jax import lax
from jax.experimental import pallas as pl
from jax.experimental.pallas import tpu as pltpu
from jax.sharding import PartitionSpec as P

TRAIN_TASKS = 12
TRAIN_PER = 32
VAL_TASKS = 8
VAL_PER = 16
TRAIN = 384
VAL = 128
CORES = 2
YS = 2

epsilon = 1e-06
FULL = 32000.0


def row_scale(v):
    top = jnp.max(jnp.abs(v), axis=1, keepdims=True)
    return jnp.maximum(top, 1e-30)


def to_int16(v, top):
    return jnp.floor(v * (FULL / top) + 0.5).astype(jnp.int32).astype(jnp.int16)


def to_lanes(top):
    rows = top.shape[0]
    return jnp.transpose(jnp.broadcast_to(top * (1.0 / FULL), (rows, 128)))[0:1]


def to_rows(lanes):
    return jnp.transpose(jnp.broadcast_to(lanes, (128, 128)))


def kernel(
    zs, pairs_ref, g_in, owner_ref, train_ref, val_ref, p_ref,
    unit_ref, tile_ref, score_ref,
    g_ref, s_ref, gram_ref, count_own, count_recv,
    p_buf, c_send, c_recv, y_own, y_send, y_recv, ys_send, ys_recv,
    z_send, z_recv, zs_send, zs_recv, acc, squares, turned,
    u_send, u_all, g_part, g_recv, g_sum,
    p_sem, cs_sem, cr_sem, yss_sem, ysr_sem, yds_sem, ydr_sem,
    zss_sem, zsr_sem, zds_sem, zdr_sem, us_sem, ur_sem, gs_sem, gr_sem, hs_sem, hr_sem, ns_sem, nr_sem,
):
    n = zs * YS * CORES
    chunks, rows, width = acc.shape
    me = lax.axis_index("param")
    core = lax.rem(me, CORES)
    y = lax.rem(lax.div(me, CORES), YS)
    z = lax.div(me, CORES * YS)
    sibling = me + 1 - 2 * core
    y_peer = me + CORES * (1 - 2 * y)
    half = g_ref.shape[0] // 2
    quarter = half // 2

    def load(k):
        return pltpu.make_async_copy(
            p_ref.at[:, pl.ds(pl.multiple_of(k * width, width), width)], p_buf.at[k], p_sem.at[k])

    def start_load(k, carry):
        load(k).start()
        return carry

    lax.fori_loop(0, chunks, start_load, 0)

    barrier = pltpu.get_barrier_semaphore()
    for j in range(1, n):
        pl.semaphore_signal(barrier, inc=1, device_id={"param": lax.rem(me + j, n)},
                            device_id_type=pl.DeviceIdType.MESH)
    pl.semaphore_wait(barrier, n - 1)

    def number(shape, axis):
        return lax.broadcasted_iota(jnp.int32, shape, axis)

    def ones_where(condition):
        return jnp.where(condition, 1.0, 0.0)

    def remote(src, dst, send, recv, to):
        return pltpu.make_async_remote_copy(
            src_ref=src, dst_ref=dst, send_sem=send, recv_sem=recv,
            device_id={"param": to}, device_id_type=pl.DeviceIdType.MESH)

    count = jnp.zeros(count_own.shape, jnp.float32)
    for i in range(pairs_ref.shape[0]):
        count = count + ones_where(
            (number(count.shape, 0) == pairs_ref[i, 0])
            & (number(count.shape, 1) >> (VAL_PER.bit_length() - 1) == pairs_ref[i, 1]))
    count_own[...] = count

    def n_copy(j):
        to = lax.rem(me + j, n)
        return remote(count_own, count_recv.at[j - 1], ns_sem.at[j - 1], nr_sem.at[j - 1], to)

    for j in range(1, n):
        n_copy(j).start()

    total_rows = g_in.shape[0]
    line = number((total_rows, 1), 0)
    bit = rows.bit_length() - 1
    zbit = zs.bit_length() - 1
    slot = (((line >> bit) & (zs - 1)) * 4 + ((line >> (bit + zbit)) & 1) * 2
            + (line >> (bit + zbit + 1))) * rows + (line & (rows - 1))
    pick = ones_where(slot == owner_ref[...]).astype(jnp.bfloat16)
    g_ref[...] = jnp.dot(pick, g_in[...], preferred_element_type=jnp.float32).astype(jnp.bfloat16)

    def place(task, per, tasks):
        size = task.shape[1]
        held = ones_where(number((tasks, size), 0) == task)
        below = ones_where(number((size, size), 0) < number((size, size), 1))
        before = jnp.dot(held.astype(jnp.bfloat16), below.astype(jnp.bfloat16),
                         preferred_element_type=jnp.float32)
        rank = jnp.sum(held * before, axis=0, keepdims=True).astype(jnp.int32)
        return task * per + rank

    spot_t = place(train_ref[...], TRAIN_PER, 16)
    spot_v = place(val_ref[...], VAL_PER, 16) + TRAIN
    by_slot = ones_where(line == owner_ref[...]).astype(jnp.bfloat16)
    spot = jnp.concatenate([spot_t, spot_v], axis=1)
    by_spot = ones_where(line == spot).astype(jnp.bfloat16)
    s_ref[...] = lax.dot_general(by_spot, by_slot, (((1,), (1,)), ((), ())),
                                 preferred_element_type=jnp.float32).astype(jnp.bfloat16)

    def core_copy(k):
        return remote(c_send.at[k], c_recv.at[k], cs_sem.at[k], cr_sem.at[k], sibling)

    def y_copies(k):
        return (remote(y_send.at[k], y_recv.at[k], yds_sem.at[k], ydr_sem.at[k], y_peer),
                remote(ys_send.at[k], ys_recv.at[k], yss_sem.at[k], ysr_sem.at[k], y_peer))

    def z_copies(k, j):
        zz = lax.rem(z + j, zs)
        to = zz * (CORES * YS) + y * CORES + core
        return (remote(z_send.at[k, zz], z_recv.at[k, j - 1], zds_sem.at[k, j - 1],
                       zdr_sem.at[k, j - 1], to),
                remote(zs_send.at[k], zs_recv.at[k, j - 1], zss_sem.at[k, j - 1],
                       zsr_sem.at[k, j - 1], to))

    squares[...] = jnp.zeros_like(squares)

    def step(t, carry):
        @pl.when(t < chunks)
        def _():
            k = t
            load(k).wait()
            theirs = g_ref[pl.ds(pl.multiple_of((1 - core) * half, half), half), :]
            c_send[k] = jnp.dot(theirs, p_buf[k], preferred_element_type=jnp.float32)
            core_copy(k).start()

        @pl.when(jnp.logical_and(t >= 1, t < chunks + 1))
        def _():
            k = t - 1
            away = pl.multiple_of((1 - y) * quarter, quarter)
            home = pl.multiple_of(y * quarter, quarter)
            base = core * half
            g_away = g_ref[pl.ds(pl.multiple_of(base + away, quarter), quarter), :]
            g_home = g_ref[pl.ds(pl.multiple_of(base + home, quarter), quarter), :]
            d_away = jnp.dot(g_away, p_buf[k], preferred_element_type=jnp.float32)
            d_home = jnp.dot(g_home, p_buf[k], preferred_element_type=jnp.float32)
            core_copy(k).wait_recv()
            v = d_away + c_recv[k, pl.ds(away, quarter), :]
            top = row_scale(v)
            y_send[k] = to_int16(v, top)
            ys_send[k] = to_lanes(top)
            for c in y_copies(k):
                c.start()
            y_own[k] = d_home + c_recv[k, pl.ds(home, quarter), :]

        @pl.when(jnp.logical_and(t >= 3, t < chunks + 3))
        def _():
            k = t - 3
            for c in y_copies(k):
                c.wait_recv()
            scale = to_rows(ys_recv[k])[:, 0:1]
            v = y_own[k] + y_recv[k].astype(jnp.int32).astype(jnp.float32) * scale
            top = row_scale(v)
            q = to_int16(v, top)
            z_send[k] = q.reshape(zs, rows, width)
            zs_send[k] = to_lanes(top)
            for j in range(1, zs):
                for c in z_copies(k, j):
                    c.start()
            y_own[k] = v
            acc[k] = y_own[k, pl.ds(pl.multiple_of(z * rows, rows), rows), :]

        @pl.when(t >= 5)
        def _():
            k = t - 5
            v = acc[k]
            for j in range(1, zs):
                for c in z_copies(k, j):
                    c.wait_recv()
                turned[...] = to_rows(zs_recv[k, j - 1])
                scale = turned[pl.ds(pl.multiple_of(z * rows, rows), rows), :][:, 0:1]
                v = v + z_recv[k, j - 1].astype(jnp.int32).astype(jnp.float32) * scale
            acc[k] = v
            squares[...] += jnp.sum(v * v, axis=1, keepdims=True)

        return carry

    lax.fori_loop(0, chunks + 5, step, 0)

    factor = lax.rsqrt(squares[...] + epsilon)[:, 0:1]
    for k in range(chunks):
        u = (acc[k] * factor).astype(jnp.bfloat16)
        unit_ref[:, k * width:(k + 1) * width] = u
        u_send[k] = u

    def u_copy(j):
        to = lax.rem(me + j, n)
        return remote(u_send.at[to], u_all.at[me], us_sem.at[j - 1], ur_sem.at[j - 1], to)

    for j in range(1, n):
        u_copy(j).start()
    u_all[me] = u_send[me]

    def drain(k, carry):
        core_copy(k).wait_send()
        for c in y_copies(k):
            c.wait_send()
        for j in range(1, zs):
            for c in z_copies(k, j):
                c.wait_send()
        return carry

    lax.fori_loop(0, chunks, drain, 0)
    for j in range(1, n):
        u_copy(j).wait()

    whole = u_all[...].reshape(n * rows, width)
    ordered = jnp.dot(s_ref[...], whole, preferred_element_type=jnp.float32).astype(jnp.bfloat16)
    gram = lax.dot_general(ordered[:TRAIN], ordered[TRAIN:], (((1,), (1,)), ((), ())),
                           preferred_element_type=jnp.float32)
    g_part[...] = gram.reshape(g_part.shape)

    def g_copy(j):
        to = lax.rem(me + j, n)
        return remote(g_part.at[to], g_recv.at[j - 1], gs_sem.at[j - 1], gr_sem.at[j - 1], to)

    for j in range(1, n):
        g_copy(j).start()
    total = g_part[me]
    for j in range(1, n):
        g_copy(j).wait_recv()
        total = total + g_recv[j - 1]
    g_sum[...] = total

    def h_copy(j):
        to = lax.rem(me + j, n)
        return remote(g_sum, gram_ref.at[me], hs_sem.at[j - 1], hr_sem.at[j - 1], to)

    for j in range(1, n):
        h_copy(j).start()
    gram_ref[me] = total
    for j in range(1, n):
        g_copy(j).wait_send()
        h_copy(j).wait()
        n_copy(j).wait()

    count = count_own[...]
    for j in range(1, n):
        count = count + count_recv[j - 1]
    gram = gram_ref[...].reshape(TRAIN_TASKS, TRAIN_PER, VAL)
    weighted = (gram * count[:TRAIN_TASKS][:, None, :]).reshape(TRAIN, VAL)
    by_train = jnp.sum(weighted, axis=1, keepdims=True) * (1.0 / VAL_PER)
    by_val = jnp.sum(weighted, axis=0, keepdims=True) * (1.0 / TRAIN_PER)
    by_val = jnp.transpose(jnp.broadcast_to(by_val, (VAL, VAL)))[:, 0:1]
    score_ref[...] = (
        jnp.sum(s_ref[:TRAIN, :].astype(jnp.float32) * by_train, axis=0, keepdims=True)
        + jnp.sum(s_ref[TRAIN:, :].astype(jnp.float32) * by_val, axis=0, keepdims=True))
    whole_gram = gram_ref[...].reshape(TRAIN_TASKS, TRAIN_PER, VAL)
    for i in range(pairs_ref.shape[0]):
        left = jnp.zeros((TRAIN_PER, VAL), jnp.float32)
        for a in range(TRAIN_TASKS):
            left = left + jnp.where(pairs_ref[i, 0] == a, whole_gram[a], 0.0)
        chosen = ones_where(number((VAL, VAL_PER), 0)
                            == number((VAL, VAL_PER), 1) + pairs_ref[i, 1] * VAL_PER)
        tile_ref[i] = jnp.dot(left, chosen, preferred_element_type=jnp.float32,
                              precision=lax.Precision.HIGHEST)


def project(n, gradients, proj_matrix, train_task, val_task, task_pairs, owner_slot):
    zs = n // (CORES * YS)
    total, depth = gradients.shape
    cols = proj_matrix.shape[1]
    rows, width, chunks = total // n, cols // n, n
    half, quarter = total // 2, total // 4
    f32, bf16, i16 = jnp.float32, jnp.bfloat16, jnp.int16
    dma = pltpu.SemaphoreType.DMA
    part = TRAIN // n
    pairs = task_pairs.shape[0]
    vmem = pl.BlockSpec(memory_space=pltpu.VMEM)
    return pl.pallas_call(
        functools.partial(kernel, zs),
        out_shape=(jax.ShapeDtypeStruct((rows, cols), bf16),
                   jax.ShapeDtypeStruct((pairs, TRAIN_PER, VAL_PER), f32),
                   jax.ShapeDtypeStruct((1, total), f32)),
        in_specs=[pl.BlockSpec(memory_space=pltpu.SMEM), vmem, vmem, vmem, vmem,
                  pl.BlockSpec(memory_space=pl.ANY)],
        out_specs=(vmem, vmem, vmem),
        scratch_shapes=[
            pltpu.VMEM((total, depth), bf16),
            pltpu.VMEM((total, total), bf16),
            pltpu.VMEM((n, part, VAL), f32),
            pltpu.VMEM((16, VAL), f32),
            pltpu.VMEM((n - 1, 16, VAL), f32),
            pltpu.VMEM((chunks, depth, width), bf16),
            pltpu.VMEM((chunks, half, width), f32),
            pltpu.VMEM((chunks, half, width), f32),
            pltpu.VMEM((chunks, quarter, width), f32),
            pltpu.VMEM((chunks, quarter, width), i16),
            pltpu.VMEM((chunks, quarter, width), i16),
            pltpu.VMEM((chunks, 1, quarter), f32),
            pltpu.VMEM((chunks, 1, quarter), f32),
            pltpu.VMEM((chunks, zs, rows, width), i16),
            pltpu.VMEM((chunks, zs - 1, rows, width), i16),
            pltpu.VMEM((chunks, 1, quarter), f32),
            pltpu.VMEM((chunks, zs - 1, 1, quarter), f32),
            pltpu.VMEM((chunks, rows, width), f32),
            pltpu.VMEM((rows, 128), f32),
            pltpu.VMEM((128, 128), f32),
            pltpu.VMEM((n, rows, width), bf16),
            pltpu.VMEM((n, rows, width), bf16),
            pltpu.VMEM((n, part, VAL), f32),
            pltpu.VMEM((n - 1, part, VAL), f32),
            pltpu.VMEM((part, VAL), f32),
            dma((chunks,)),
            dma((chunks,)), dma((chunks,)),
            dma((chunks,)), dma((chunks,)), dma((chunks,)), dma((chunks,)),
            dma((chunks, zs - 1)), dma((chunks, zs - 1)),
            dma((chunks, zs - 1)), dma((chunks, zs - 1)),
            dma((n - 1,)), dma((n - 1,)), dma((n - 1,)), dma((n - 1,)),
            dma((n - 1,)), dma((n - 1,)), dma((n - 1,)), dma((n - 1,)),
        ],
        compiler_params=pltpu.CompilerParams(
            collective_id=0, has_side_effects=True, vmem_limit_bytes=60 * 2**20),
        cost_estimate=pl.CostEstimate(
            flops=2 * total * depth * cols, bytes_accessed=2 * depth * cols, transcendentals=0),
    )(task_pairs, gradients, owner_slot.reshape(1, -1), train_task.reshape(1, -1),
      val_task.reshape(1, -1), proj_matrix)


def fused(n, gradients, proj_matrix, train_task, val_task, task_pairs, owner_slot):
    rows = gradients.shape[0] // n
    unit_rows, tiles, scores = project(
        n, gradients, proj_matrix, train_task, val_task, task_pairs, owner_slot)
    mine = lax.dynamic_slice(scores, (0, lax.axis_index("param") * rows), (1, rows))
    return (unit_rows, tiles, mine.reshape(rows))


def shards(gradients, proj_matrix, train_task, val_task, task_pairs, owner_slot):
    total_rows = gradients.shape[0]
    inverse = (
        jnp.zeros((total_rows,), jnp.int32)
        .at[owner_slot]
        .set(jnp.arange(total_rows, dtype=jnp.int32))
    )
    ordered = gradients[inverse]
    owned = lax.psum_scatter(
        jnp.dot(ordered, proj_matrix, preferred_element_type=jnp.float32),
        "param",
        scatter_dimension=0,
        tiled=True,
    )
    squares = jnp.sum(owned * owned, axis=1, keepdims=True)
    unit_rows = (owned * lax.rsqrt(squares + epsilon)).astype(jnp.bfloat16)
    train_rows = jnp.argsort(train_task, stable=True).reshape(TRAIN_TASKS, TRAIN_PER)
    val_order = jnp.argsort(val_task, stable=True).reshape(VAL_TASKS, VAL_PER)
    left_slots = owner_slot[train_rows[task_pairs[:, 0]]]
    val_index = val_order[task_pairs[:, 1]]
    right_slots = owner_slot[val_index + TRAIN]
    every_unit = lax.all_gather(unit_rows, "param", axis=0, tiled=True)
    left_side = every_unit[left_slots]
    right_side = every_unit[right_slots]
    tiles = jnp.einsum("prk,pck->prc", left_side, right_side, preferred_element_type=jnp.float32)
    contrib = jnp.zeros((total_rows,), jnp.float32)
    contrib = contrib.at[left_slots].add(jnp.mean(tiles, axis=2))
    contrib = contrib.at[right_slots].add(jnp.mean(tiles, axis=1))
    scores = lax.psum_scatter(contrib, "param", scatter_dimension=0, tiled=True)
    return (unit_rows, tiles, scores)


def solution(mesh):
    in_specs = (
        P("groups", "param"),
        P("param", None),
        P("groups"),
        P("groups"),
        P(("groups", "param"), None),
        P("groups"),
    )
    out_specs = (
        P(("groups", "param"), None),
        P(("groups", "param"), None, None),
        P(("groups", "param")),
    )
    n = mesh.shape["param"]
    body = functools.partial(fused, n) if n == 16 else shards
    return jax.shard_map(body, mesh=mesh, in_specs=in_specs, out_specs=out_specs, check_vma=False)
```

```python
import functools

import jax
import jax.numpy as jnp
from jax import lax
from jax.experimental import pallas as pl
from jax.experimental.pallas import tpu as pltpu
from jax.sharding import PartitionSpec as P

TRAIN_TASKS = 12
TRAIN_PER = 32
VAL_TASKS = 8
VAL_PER = 16
TRAIN = 384
VAL = 128
CORES = 2
YS = 2

epsilon = 1e-06
FULL = 32000.0


def row_scale(v):
    top = jnp.max(jnp.abs(v), axis=1, keepdims=True)
    return jnp.maximum(top, 1e-30)


def to_int16(v, top):
    return jnp.floor(v * (FULL / top) + 0.5).astype(jnp.int32).astype(jnp.int16)


def to_lanes(top):
    rows = top.shape[0]
    return jnp.transpose(jnp.broadcast_to(top * (1.0 / FULL), (rows, 128)))[0:1]


def to_rows(lanes):
    return jnp.transpose(jnp.broadcast_to(lanes, (128, 128)))


def kernel(
    zs, pairs_ref, g_in, owner_ref, train_ref, val_ref, p_ref,
    unit_ref, tile_ref, score_ref,
    g_ref, s_ref, gram_ref, count_own, count_recv,
    p_buf, c_send, c_recv, y_own, y_send, y_recv, ys_send, ys_recv,
    z_own, z_send, z_recv, zs_send, zs_recv, w_send, w_recv, ws_send, ws_recv, acc, squares, turned,
    u_send, u_all, g_part, g_recv, g_sum,
    p_sem, cs_sem, cr_sem, yss_sem, ysr_sem, yds_sem, ydr_sem,
    zss_sem, zsr_sem, zds_sem, zdr_sem, wss_sem, wsr_sem, wds_sem, wdr_sem, us_sem, ur_sem, gs_sem, gr_sem, hs_sem, hr_sem, ns_sem, nr_sem,
):
    n = zs * YS * CORES
    chunks, rows, width = acc.shape
    me = lax.axis_index("param")
    core = lax.rem(me, CORES)
    y = lax.rem(lax.div(me, CORES), YS)
    z = lax.div(me, CORES * YS)
    sibling = me + 1 - 2 * core
    y_peer = me + CORES * (1 - 2 * y)
    near = lax.rem(z, 2)
    far = lax.div(z, 2)
    z_peer = me + CORES * YS * (1 - 2 * near)
    w_peer = me + CORES * YS * 2 * (1 - 2 * far)
    half = g_in.shape[0] // 2
    quarter = half // 2
    eighth = quarter // 2

    def swapped(k):
        return lax.rem(k, 2)

    def first(k):
        return y + (near - y) * swapped(k)

    def second(k):
        return near + (y - near) * swapped(k)

    def load(k):
        return pltpu.make_async_copy(
            p_ref.at[:, pl.ds(pl.multiple_of(k * width, width), width)], p_buf.at[k], p_sem.at[k])

    def start_load(k, carry):
        load(k).start()
        return carry

    lax.fori_loop(0, chunks, start_load, 0)

    barrier = pltpu.get_barrier_semaphore()
    for j in range(1, n):
        pl.semaphore_signal(barrier, inc=1, device_id={"param": lax.rem(me + j, n)},
                            device_id_type=pl.DeviceIdType.MESH)
    pl.semaphore_wait(barrier, n - 1)

    def number(shape, axis):
        return lax.broadcasted_iota(jnp.int32, shape, axis)

    def ones_where(condition):
        return jnp.where(condition, 1.0, 0.0)

    def remote(src, dst, send, recv, to):
        return pltpu.make_async_remote_copy(
            src_ref=src, dst_ref=dst, send_sem=send, recv_sem=recv,
            device_id={"param": to}, device_id_type=pl.DeviceIdType.MESH)

    count = jnp.zeros(count_own.shape, jnp.float32)
    for i in range(pairs_ref.shape[0]):
        count = count + ones_where(
            (number(count.shape, 0) == pairs_ref[i, 0])
            & (number(count.shape, 1) >> (VAL_PER.bit_length() - 1) == pairs_ref[i, 1]))
    count_own[...] = count

    def n_copy(j):
        to = lax.rem(me + j, n)
        return remote(count_own, count_recv.at[j - 1], ns_sem.at[j - 1], nr_sem.at[j - 1], to)

    for j in range(1, n):
        n_copy(j).start()

    total_rows = g_in.shape[0]
    line = number((total_rows, 1), 0)
    bit = rows.bit_length() - 1
    for i in range(2):
        b_first = (line >> (bit + 2)) & 1
        b_second = (line >> (bit + 1)) & 1
        line_y, line_near = (b_first, b_second) if i == 0 else (b_second, b_first)
        slot = (((line >> bit) & 1) * 8 + line_near * 4 + line_y * 2
                + (line >> (bit + 3))) * rows + (line & (rows - 1))
        pick = ones_where(slot == owner_ref[...]).astype(jnp.bfloat16)
        g_ref[i] = jnp.dot(pick, g_in[...], preferred_element_type=jnp.float32).astype(jnp.bfloat16)

    def place(task, per, tasks):
        size = task.shape[1]
        held = ones_where(number((tasks, size), 0) == task)
        below = ones_where(number((size, size), 0) < number((size, size), 1))
        before = jnp.dot(held.astype(jnp.bfloat16), below.astype(jnp.bfloat16),
                         preferred_element_type=jnp.float32)
        rank = jnp.sum(held * before, axis=0, keepdims=True).astype(jnp.int32)
        return task * per + rank

    train = jnp.concatenate([train_ref[i:i + 1] for i in range(train_ref.shape[0])], axis=1)
    spot_t = place(train, TRAIN_PER, 16)
    spot_v = place(val_ref[...], VAL_PER, 16) + TRAIN
    by_slot = ones_where(line == owner_ref[...]).astype(jnp.bfloat16)
    spot = jnp.concatenate([spot_t, spot_v], axis=1)
    by_spot = ones_where(line == spot).astype(jnp.bfloat16)
    s_ref[...] = lax.dot_general(by_spot, by_slot, (((1,), (1,)), ((), ())),
                                 preferred_element_type=jnp.float32).astype(jnp.bfloat16)

    def core_copy(k):
        return remote(c_send.at[k], c_recv.at[k], cs_sem.at[k], cr_sem.at[k], sibling)

    def y_copies(k):
        to = y_peer + (z_peer - y_peer) * swapped(k)
        return (remote(y_send.at[k], y_recv.at[k], yds_sem.at[k], ydr_sem.at[k], to),
                remote(ys_send.at[k], ys_recv.at[k], yss_sem.at[k], ysr_sem.at[k], to))

    def z_copies(k):
        to = z_peer + (y_peer - z_peer) * swapped(k)
        return (remote(z_send.at[k, 1 - second(k)], z_recv.at[k], zds_sem.at[k], zdr_sem.at[k], to),
                remote(zs_send.at[k], zs_recv.at[k], zss_sem.at[k], zsr_sem.at[k], to))

    def w_copies(k):
        return (remote(w_send.at[k, 1 - far], w_recv.at[k], wds_sem.at[k], wdr_sem.at[k], w_peer),
                remote(ws_send.at[k], ws_recv.at[k], wss_sem.at[k], wsr_sem.at[k], w_peer))

    squares[...] = jnp.zeros_like(squares)

    def step(t, carry):
        @pl.when(t < chunks)
        def _():
            k = t
            load(k).wait()
            theirs = g_ref[swapped(k), pl.ds(pl.multiple_of((1 - core) * half, half), half), :]
            c_send[k] = jnp.dot(theirs, p_buf[k], preferred_element_type=jnp.float32)
            core_copy(k).start()

        @pl.when(jnp.logical_and(t >= 1, t < chunks + 1))
        def _():
            k = t - 1
            away = pl.multiple_of((1 - first(k)) * quarter, quarter)
            home = pl.multiple_of(first(k) * quarter, quarter)
            base = core * half
            g_away = g_ref[swapped(k), pl.ds(pl.multiple_of(base + away, quarter), quarter), :]
            g_home = g_ref[swapped(k), pl.ds(pl.multiple_of(base + home, quarter), quarter), :]
            d_away = jnp.dot(g_away, p_buf[k], preferred_element_type=jnp.float32)
            d_home = jnp.dot(g_home, p_buf[k], preferred_element_type=jnp.float32)
            core_copy(k).wait_recv()
            v = d_away + c_recv[k, pl.ds(away, quarter), :]
            top = row_scale(v)
            y_send[k] = to_int16(v, top)
            ys_send[k] = to_lanes(top)
            for c in y_copies(k):
                c.start()
            y_own[k] = d_home + c_recv[k, pl.ds(home, quarter), :]

        @pl.when(jnp.logical_and(t >= 3, t < chunks + 3))
        def _():
            k = t - 3
            for c in y_copies(k):
                c.wait_recv()
            scale = to_rows(ys_recv[k])[:, 0:1]
            v = y_own[k] + y_recv[k].astype(jnp.int32).astype(jnp.float32) * scale
            top = row_scale(v)
            z_send[k] = to_int16(v, top).reshape(2, eighth, width)
            zs_send[k] = to_lanes(top)
            for c in z_copies(k):
                c.start()
            z_own[k] = v.reshape(2, eighth, width)

        @pl.when(jnp.logical_and(t >= 5, t < chunks + 5))
        def _():
            k = t - 5
            for c in z_copies(k):
                c.wait_recv()
            turned[...] = to_rows(zs_recv[k])
            at = pl.multiple_of(second(k) * eighth, eighth)
            scale = turned[pl.ds(at, eighth), :][:, 0:1]
            v = z_own[k, second(k)] + z_recv[k].astype(jnp.int32).astype(jnp.float32) * scale
            top = row_scale(v)
            w_send[k] = to_int16(v, top).reshape(2, rows, width)
            ws_send[k] = to_lanes(jnp.concatenate([top, top], axis=0))
            for c in w_copies(k):
                c.start()
            z_own[k, 0] = v
            acc[k] = z_own[k, 0, pl.ds(pl.multiple_of(far * rows, rows), rows), :]

        @pl.when(t >= 7)
        def _():
            k = t - 7
            for c in w_copies(k):
                c.wait_recv()
            turned[...] = to_rows(ws_recv[k])
            scale = turned[pl.ds(pl.multiple_of(far * rows, rows), rows), :][:, 0:1]
            v = acc[k] + w_recv[k].astype(jnp.int32).astype(jnp.float32) * scale
            acc[k] = v
            squares[...] += jnp.sum(v * v, axis=1, keepdims=True)

        return carry

    lax.fori_loop(0, chunks + 7, step, 0)

    factor = lax.rsqrt(squares[...] + epsilon)[:, 0:1]
    for k in range(chunks):
        u = (acc[k] * factor).astype(jnp.bfloat16)
        unit_ref[:, k * width:(k + 1) * width] = u
        u_send[k] = u

    def u_copy(j):
        to = lax.rem(me + j, n)
        return remote(u_send.at[to], u_all.at[me], us_sem.at[j - 1], ur_sem.at[j - 1], to)

    for j in range(1, n):
        u_copy(j).start()
    u_all[me] = u_send[me]

    def drain(k, carry):
        core_copy(k).wait_send()
        for c in y_copies(k):
            c.wait_send()
        for c in z_copies(k):
            c.wait_send()
        for c in w_copies(k):
            c.wait_send()
        return carry

    lax.fori_loop(0, chunks, drain, 0)
    for j in range(1, n):
        u_copy(j).wait()

    whole = u_all[...].reshape(n * rows, width)
    ordered = jnp.dot(s_ref[...], whole, preferred_element_type=jnp.float32).astype(jnp.bfloat16)
    gram = lax.dot_general(ordered[:TRAIN], ordered[TRAIN:], (((1,), (1,)), ((), ())),
                           preferred_element_type=jnp.float32)
    g_part[...] = gram.reshape(g_part.shape)

    def g_copy(j):
        to = lax.rem(me + j, n)
        return remote(g_part.at[to], g_recv.at[j - 1], gs_sem.at[j - 1], gr_sem.at[j - 1], to)

    for j in range(1, n):
        g_copy(j).start()
    total = g_part[me]
    for j in range(1, n):
        g_copy(j).wait_recv()
        total = total + g_recv[j - 1]
    g_sum[...] = total

    def h_copy(j):
        to = lax.rem(me + j, n)
        return remote(g_sum, gram_ref.at[me], hs_sem.at[j - 1], hr_sem.at[j - 1], to)

    for j in range(1, n):
        h_copy(j).start()
    gram_ref[me] = total
    for j in range(1, n):
        g_copy(j).wait_send()
        h_copy(j).wait()
        n_copy(j).wait()

    count = count_own[...]
    for j in range(1, n):
        count = count + count_recv[j - 1]
    gram = gram_ref[...].reshape(TRAIN_TASKS, TRAIN_PER, VAL)
    weighted = (gram * count[:TRAIN_TASKS][:, None, :]).reshape(TRAIN, VAL)
    by_train = jnp.sum(weighted, axis=1, keepdims=True) * (1.0 / VAL_PER)
    by_val = jnp.sum(weighted, axis=0, keepdims=True) * (1.0 / TRAIN_PER)
    by_val = jnp.transpose(jnp.broadcast_to(by_val, (VAL, VAL)))[:, 0:1]
    score_ref[...] = (
        jnp.sum(s_ref[:TRAIN, :].astype(jnp.float32) * by_train, axis=0, keepdims=True)
        + jnp.sum(s_ref[TRAIN:, :].astype(jnp.float32) * by_val, axis=0, keepdims=True))
    whole_gram = gram_ref[...].reshape(TRAIN_TASKS, TRAIN_PER, VAL)
    for i in range(pairs_ref.shape[0]):
        left = jnp.zeros((TRAIN_PER, VAL), jnp.float32)
        for a in range(TRAIN_TASKS):
            left = left + jnp.where(pairs_ref[i, 0] == a, whole_gram[a], 0.0)
        chosen = ones_where(number((VAL_PER, VAL), 1)
                            == number((VAL_PER, VAL), 0) + pairs_ref[i, 1] * VAL_PER)
        tile_ref[i] = lax.dot_general(chosen, left, (((1,), (1,)), ((), ())),
                                      preferred_element_type=jnp.float32,
                                      precision=lax.Precision.HIGHEST)


def project(n, gradients, proj_matrix, train_task, val_task, task_pairs, owner_slot):
    zs = n // (CORES * YS)
    total, depth = gradients.shape
    cols = proj_matrix.shape[1]
    rows, width, chunks = total // n, cols // n, n
    half, quarter = total // 2, total // 4
    f32, bf16, i16 = jnp.float32, jnp.bfloat16, jnp.int16
    dma = pltpu.SemaphoreType.DMA
    part = TRAIN // n
    pairs = task_pairs.shape[0]
    vmem = pl.BlockSpec(memory_space=pltpu.VMEM)
    return pl.pallas_call(
        functools.partial(kernel, zs),
        out_shape=(jax.ShapeDtypeStruct((rows, cols), bf16),
                   jax.ShapeDtypeStruct((pairs, VAL_PER, TRAIN_PER), f32),
                   jax.ShapeDtypeStruct((1, total), f32)),
        in_specs=[pl.BlockSpec(memory_space=pltpu.SMEM), vmem, vmem, vmem, vmem,
                  pl.BlockSpec(memory_space=pl.ANY)],
        out_specs=(vmem, vmem, vmem),
        scratch_shapes=[
            pltpu.VMEM((2, total, depth), bf16),
            pltpu.VMEM((total, total), bf16),
            pltpu.VMEM((n, part, VAL), f32),
            pltpu.VMEM((16, VAL), f32),
            pltpu.VMEM((n - 1, 16, VAL), f32),
            pltpu.VMEM((chunks, depth, width), bf16),
            pltpu.VMEM((chunks, half, width), f32),
            pltpu.VMEM((chunks, half, width), f32),
            pltpu.VMEM((chunks, quarter, width), f32),
            pltpu.VMEM((chunks, quarter, width), i16),
            pltpu.VMEM((chunks, quarter, width), i16),
            pltpu.VMEM((chunks, 1, quarter), f32),
            pltpu.VMEM((chunks, 1, quarter), f32),
            pltpu.VMEM((chunks, 2, quarter // 2, width), f32),
            pltpu.VMEM((chunks, 2, quarter // 2, width), i16),
            pltpu.VMEM((chunks, quarter // 2, width), i16),
            pltpu.VMEM((chunks, 1, quarter), f32),
            pltpu.VMEM((chunks, 1, quarter), f32),
            pltpu.VMEM((chunks, 2, rows, width), i16),
            pltpu.VMEM((chunks, rows, width), i16),
            pltpu.VMEM((chunks, 1, quarter), f32),
            pltpu.VMEM((chunks, 1, quarter), f32),
            pltpu.VMEM((chunks, rows, width), f32),
            pltpu.VMEM((rows, 128), f32),
            pltpu.VMEM((128, 128), f32),
            pltpu.VMEM((n, rows, width), bf16),
            pltpu.VMEM((n, rows, width), bf16),
            pltpu.VMEM((n, part, VAL), f32),
            pltpu.VMEM((n - 1, part, VAL), f32),
            pltpu.VMEM((part, VAL), f32),
            dma((chunks,)),
            dma((chunks,)), dma((chunks,)),
            dma((chunks,)), dma((chunks,)), dma((chunks,)), dma((chunks,)),
            dma((chunks,)), dma((chunks,)), dma((chunks,)), dma((chunks,)),
            dma((chunks,)), dma((chunks,)), dma((chunks,)), dma((chunks,)),
            dma((n - 1,)), dma((n - 1,)), dma((n - 1,)), dma((n - 1,)),
            dma((n - 1,)), dma((n - 1,)), dma((n - 1,)), dma((n - 1,)),
        ],
        compiler_params=pltpu.CompilerParams(
            collective_id=0, has_side_effects=True, vmem_limit_bytes=60 * 2**20),
        cost_estimate=pl.CostEstimate(
            flops=2 * total * depth * cols, bytes_accessed=2 * depth * cols, transcendentals=0),
    )(task_pairs, gradients, owner_slot.reshape(1, -1), train_task.reshape(-1, 128),
      val_task.reshape(1, -1), proj_matrix)


def fused(n, gradients, proj_matrix, train_task, val_task, task_pairs, owner_slot):
    rows = gradients.shape[0] // n
    unit_rows, tiles, scores = project(
        n, gradients, proj_matrix, train_task, val_task, task_pairs, owner_slot)
    mine = lax.dynamic_slice(scores, (0, lax.axis_index("param") * rows), (1, rows))
    return (unit_rows, tiles.transpose(0, 2, 1), mine.reshape(rows))


def shards(gradients, proj_matrix, train_task, val_task, task_pairs, owner_slot):
    total_rows = gradients.shape[0]
    inverse = (
        jnp.zeros((total_rows,), jnp.int32)
        .at[owner_slot]
        .set(jnp.arange(total_rows, dtype=jnp.int32))
    )
    ordered = gradients[inverse]
    owned = lax.psum_scatter(
        jnp.dot(ordered, proj_matrix, preferred_element_type=jnp.float32),
        "param",
        scatter_dimension=0,
        tiled=True,
    )
    squares = jnp.sum(owned * owned, axis=1, keepdims=True)
    unit_rows = (owned * lax.rsqrt(squares + epsilon)).astype(jnp.bfloat16)
    train_rows = jnp.argsort(train_task, stable=True).reshape(TRAIN_TASKS, TRAIN_PER)
    val_order = jnp.argsort(val_task, stable=True).reshape(VAL_TASKS, VAL_PER)
    left_slots = owner_slot[train_rows[task_pairs[:, 0]]]
    val_index = val_order[task_pairs[:, 1]]
    right_slots = owner_slot[val_index + TRAIN]
    every_unit = lax.all_gather(unit_rows, "param", axis=0, tiled=True)
    left_side = every_unit[left_slots]
    right_side = every_unit[right_slots]
    tiles = jnp.einsum("prk,pck->prc", left_side, right_side, preferred_element_type=jnp.float32)
    contrib = jnp.zeros((total_rows,), jnp.float32)
    contrib = contrib.at[left_slots].add(jnp.mean(tiles, axis=2))
    contrib = contrib.at[right_slots].add(jnp.mean(tiles, axis=1))
    scores = lax.psum_scatter(contrib, "param", scatter_dimension=0, tiled=True)
    return (unit_rows, tiles, scores)


def solution(mesh):
    in_specs = (
        P("groups", "param"),
        P("param", None),
        P("groups"),
        P("groups"),
        P(("groups", "param"), None),
        P("groups"),
    )
    out_specs = (
        P(("groups", "param"), None),
        P(("groups", "param"), None, None),
        P(("groups", "param")),
    )
    n = mesh.shape["param"]
    body = functools.partial(fused, n) if n == 16 else shards
    return jax.shard_map(body, mesh=mesh, in_specs=in_specs, out_specs=out_specs, check_vma=False)
```
